256 devices in a mesh: blk: 64 (over z, x, y_lo), rep: 4 (over y_hi, core).
Axes of the slice: x: 4, y: 4 (y_hi: 2, y_lo: 2; y = y_hi * 2 + y_lo), z: 8, core: 2. Of those that a mesh axis runs over, the one named last changes fastest.
Arguments:
- row_emb: bfloat16 [65536, 300], P('blk'), may hold values from -1.796875 to 1.796875
- col_emb: bfloat16 [65536, 300], P('blk'), may hold values from -1.796875 to 1.796875
- row_acc: float32 [65536, 300], P('blk'), may hold values from 0.0003 to 0.03
- col_acc: float32 [65536, 300], P('blk'), may hold values from 0.0003 to 0.03
- row_offset: bfloat16 [65536], P('blk'), may hold values from 0.5 to 3
- col_offset: bfloat16 [65536], P('blk'), may hold values from 0.5 to 3
- counts: int32 [64, 4, 2, 1024, 1024], P('blk', 'rep'), may hold values from 0 to 1023, as said below
- row_index: int32 [64, 4, 2, 1024], P('blk', 'rep'), may hold values from 0 to 1023, as said below
- col_index: int32 [64, 4, 2, 1024], P('blk', 'rep'), may hold values from 0 to 1023, as said below
Outputs:
- new_row_emb: bfloat16 [65536, 300], P('blk')
- new_col_emb: bfloat16 [65536, 300], P('blk')
The draws below stay inside these ranges and needn't reach their ends.
Inputs may be any that keep to these rules, and one draw needn't show every extreme that they name: Every shard has some cell with count 1023, and zeros among its counts. `row_index`: each row of the last dimension lists every one of the 1024 positions once. `col_index`: each row of the last dimension lists every one of the 1024 positions once.
All inputs are finite; a program needn't handle non-finite values.
Results may differ from the reference program's by a relative error of at most 0.0031.
Values may be sent and summed in bfloat16 or wider, within the bound.
No kernel may reach another device: no remote copies, remote signals or barrier semaphores. Data moves between devices by JAX's collectives and lax.ppermute only.
A program may use at most 128 MiB of HBM per device.

```python
import math
import jax
import jax.numpy as jnp
from jax import lax

DIM = 300
SHARD = 1024
PAIRS = 2
BLOCKS = 64
REPS = 4
VOCAB = 65536


def draw_counts(key, part):
    key = jax.random.fold_in(key, 1)
    first, second = jax.random.split(key)
    shape = (BLOCKS, REPS, PAIRS, SHARD, SHARD)
    magnitude = jax.random.randint(first, shape, 0, 11)
    ceiling = jnp.left_shift(jnp.ones(shape, jnp.int32), magnitude)
    values = jax.random.randint(second, shape, 0, ceiling)
    values = values.at[:, :, :, 0, 0].set(1023)
    return values.at[:, :, :, 0, 1].set(0).astype(jnp.int32)


def permuted_rows(key):
    keys = jax.random.split(key, BLOCKS * REPS * PAIRS)
    rows = jax.vmap(lambda single: jax.random.permutation(single, SHARD))(keys)
    return rows.reshape(BLOCKS, REPS, PAIRS, SHARD).astype(jnp.int32)


def draw_row_index(key, part):
    key = jax.random.fold_in(key, 2)
    return permuted_rows(key)


def draw_col_index(key, part):
    key = jax.random.fold_in(key, 3)
    return permuted_rows(key)


def steps_of(key, dims, cuts, smallest, high):
    factor_of, own = 1.0, jax.random.fold_in(key, 6)
    for dim, shards_of in cuts:
        steps = jnp.exp(jax.random.uniform(jax.random.fold_in(own, dim), (shards_of,), jnp.float32, smallest / len(cuts), high / len(cuts)))
        factor_of = factor_of * jnp.repeat(steps, dims[dim] // shards_of).reshape([-1 if axis == dim else 1 for axis in range(len(dims))])
    return factor_of


def bell_draw(key, dims, spread, bound, cuts=(), kind=jnp.bfloat16):
    level = steps_of(key, dims, cuts, -0.22, 0.18) if cuts else 1.0
    entries = jax.random.normal(key, dims, jnp.float32) * spread * level
    return jnp.minimum(jnp.maximum(entries, -bound), bound).astype(kind)


def setup_inputs(seed: int = 0) -> dict:
    key_list = jax.random.split(jax.random.key(seed), 10)
    row_emb = bell_draw(key_list[0], (VOCAB, DIM), 0.3, 1.796875, ((0, 64),))
    col_emb = bell_draw(key_list[1], (VOCAB, DIM), 0.3, 1.796875, ((0, 64),))
    row_acc = jnp.clip(jnp.exp(math.log(0.03) - 4.6051701 * jax.random.uniform(key_list[2], (VOCAB, DIM), jnp.float32) ** steps_of(key_list[2], (VOCAB, DIM), ((0, 64),), -0.2, 0.2)), 0.0003, 0.03)
    col_acc = jnp.clip(jnp.exp(math.log(0.03) - 4.6051701 * jax.random.uniform(key_list[3], (VOCAB, DIM), jnp.float32) ** steps_of(key_list[3], (VOCAB, DIM), ((0, 64),), -0.2, 0.2)), 0.0003, 0.03)
    row_offset = jnp.clip(0.5 + 2.5 * jax.random.uniform(key_list[4], (VOCAB,), jnp.float32) ** steps_of(key_list[4], (VOCAB,), ((0, 64),), -0.2, 0.2), 0.5, 3.0).astype(jnp.bfloat16)
    col_offset = jnp.clip(0.5 + 2.5 * jax.random.uniform(key_list[5], (VOCAB,), jnp.float32) ** steps_of(key_list[5], (VOCAB,), ((0, 64),), -0.2, 0.2), 0.5, 3.0).astype(jnp.bfloat16)
    counts = draw_counts(jax.random.fold_in(key_list[9], 71), 0)
    row_index = draw_row_index(jax.random.fold_in(key_list[9], 71), 0)
    col_index = draw_col_index(jax.random.fold_in(key_list[9], 71), 0)
    return dict(row_emb=row_emb, col_emb=col_emb, row_acc=row_acc, col_acc=col_acc, row_offset=row_offset, col_offset=col_offset, counts=counts, row_index=row_index, col_index=col_index)


LEARN_RATE = 0.05

def score_shard(row_vec, col_vec, count, row_off, col_off):
    est = jnp.dot(row_vec, col_vec.T, preferred_element_type=jnp.float32)
    count_f = count.astype(jnp.float32)
    offsets = row_off.astype(jnp.float32)[:, None] + col_off.astype(jnp.float32)[None, :]
    pmi = jnp.log(jnp.maximum(count_f, 1.0)) - offsets
    confidence = 0.1 + 0.25 * jnp.sqrt(count_f)
    cells = jnp.where(count > 0, confidence * (est - pmi), jax.nn.sigmoid(est + offsets))
    cells = (cells / SHARD).astype(jnp.bfloat16)
    row_part = jnp.dot(cells, col_vec, preferred_element_type=jnp.float32)
    col_part = lax.dot_general(cells, row_vec, (((0,), (0,)), ((), ())), preferred_element_type=jnp.float32)
    return (row_part, col_part)

def adagrad(table, accum, total):
    new_acc = accum + total * total
    return (table.astype(jnp.float32) - LEARN_RATE * total / jnp.sqrt(new_acc)).astype(jnp.bfloat16)

def reference(row_emb, col_emb, row_acc, col_acc, row_offset, col_offset, counts, row_index, col_index):
    row_tab = row_emb.reshape(BLOCKS, SHARD, DIM)
    col_tab = col_emb.reshape(BLOCKS, SHARD, DIM)
    row_offs = row_offset.reshape(BLOCKS, SHARD)
    col_offs = col_offset.reshape(BLOCKS, SHARD)
    stride = BLOCKS // (2 * REPS)

    def one_block(block, carry):
        row_grad, col_grad = carry
        block = jnp.asarray(block).astype(jnp.int32)
        for replica in range(REPS):
            for pair_id in range(PAIRS):
                partner = ((block + stride * (replica + REPS * pair_id)) % BLOCKS).astype(jnp.int32)
                row_idx = row_index[block, replica, pair_id]
                col_idx = col_index[partner, replica, pair_id]
                row_part, col_part = score_shard(row_tab[block][row_idx], col_tab[partner][col_idx], counts[block, replica, pair_id], row_offs[block][row_idx], col_offs[partner][col_idx])
                row_grad = row_grad.at[block, row_idx].add(row_part)
                col_grad = col_grad.at[partner, col_idx].add(col_part)
        return (row_grad, col_grad)
    zeros = jnp.zeros((BLOCKS, SHARD, DIM), jnp.float32)
    row_grad, col_grad = lax.fori_loop(0, BLOCKS, one_block, (zeros, zeros))
    new_row = adagrad(row_emb, row_acc, row_grad.reshape(VOCAB, DIM))
    new_col = adagrad(col_emb, col_acc, col_grad.reshape(VOCAB, DIM))
    return (new_row, new_col)
```

```python
import jax
import jax.numpy as jnp
from jax import lax
from jax.experimental import pallas as pl
from jax.experimental.pallas import tpu as pltpu
from jax.sharding import PartitionSpec as P

LEARN_RATE = 0.05
DIM = 300
WIDE = 304
TERMS = 1024
HALF = TERMS // 2
TILE = 256
RING = 8
STRIDE = 8
AXES = ("blk", "rep")
F32 = jnp.float32
BF16 = jnp.bfloat16


def hop(array, moves):
    perm = []
    for blk in range(RING * STRIDE):
        for rep in range(4):
            if moves[rep] is None:
                continue
            by, to = moves[rep]
            dst = (blk + STRIDE * by) % (RING * STRIDE)
            perm.append((blk * 4 + rep, dst * 4 + to))
    return lax.ppermute(array, AXES, perm)


CORE = [(0, 1), (0, 0), (0, 3), (0, 2)]
ACROSS = [(0, 2), (0, 3), (0, 0), (0, 1)]


def dot(a, b, ca, cb):
    return lax.dot_general(a, b, (((ca,), (cb,)), ((), ())), preferred_element_type=F32)


def pack_kernel(off_row, one_row, emb_ref, off_ref, out_ref):
    pick = lax.broadcasted_iota(jnp.int32, (WIDE, DIM), 0) == lax.broadcasted_iota(
        jnp.int32, (WIDE, DIM), 1
    )
    flat = dot(jnp.where(pick, 1.0, 0.0).astype(BF16), emb_ref[...], 1, 1)
    row = lax.broadcasted_iota(jnp.int32, (WIDE, TERMS), 0)
    flat = jnp.where(row == off_row, off_ref[...].astype(F32), flat)
    out_ref[...] = jnp.where(row == one_row, 1.0, flat).astype(BF16)


def pack(emb, off, off_row, one_row):
    def kernel(*refs):
        pack_kernel(off_row, one_row, *refs)

    return pl.pallas_call(
        kernel,
        out_shape=jax.ShapeDtypeStruct((WIDE, TERMS), BF16),
        cost_estimate=pl.CostEstimate(flops=2 * WIDE * 512 * TERMS, bytes_accessed=1500000, transcendentals=0),
    )(emb, off)


def one_hot(index, terms, width):
    hit = lax.broadcasted_iota(jnp.int32, (terms, width), 0) == index
    return jnp.where(hit, 1.0, 0.0).astype(BF16)


def score_kernel(
    second, pair_ref, count_ref, row_idx_ref, col_idx_ref, row_ref, col_ref, *refs
):
    if second:
        prev_ref, row_out, col_out, col_pick, col_vec, row_acc, col_acc = refs
    else:
        row_out, col_out, col_pick, col_vec, row_acc, col_acc = refs
    step = pl.program_id(0)

    @pl.when(step == 0)
    def _():
        col_pick[...] = one_hot(col_idx_ref[...], TERMS, TERMS)
        col_vec[...] = dot(col_ref[...], col_pick[...], 1, 0).astype(BF16)
        row_acc[...] = prev_ref[...] if second else jnp.zeros_like(row_acc)
        col_acc[...] = jnp.zeros_like(col_acc)

    row_pick = one_hot(row_idx_ref[0], TERMS, TILE)
    row_vec = dot(row_ref[...], row_pick, 1, 0).astype(BF16)
    score = dot(row_vec, col_vec[...], 0, 0)
    count = count_ref[0]
    count_f = count.astype(F32)
    scale = 1.0 / TERMS
    confidence = 0.1 * scale + (0.25 * scale) * (count_f * lax.rsqrt(count_f))
    seen = confidence * (score - jnp.log(count_f))
    unseen = 0.5 * scale + (0.5 * scale) * jnp.tanh(0.5 * score)
    cells = jnp.where(count > 0, seen, unseen).astype(BF16)
    row_part = dot(col_vec[...], cells, 1, 1).astype(BF16)
    row_acc[...] += dot(row_part, row_pick, 1, 1)
    col_acc[...] += dot(row_vec, cells, 1, 0)

    @pl.when(step == pl.num_programs(0) - 1)
    def _():
        col_out[...] = dot(col_acc[...].astype(BF16), col_pick[...], 1, 1).astype(BF16)
        if second:
            row_out[0] = row_acc[:, :HALF].astype(BF16)
            row_out[1] = row_acc[:, HALF:].astype(BF16)
        else:
            row_out[...] = row_acc[...]


def score(pair, counts, row_idx, col_idx, row_pk, col_pk, prev=None):
    second = prev is not None

    def kernel(*refs):
        score_kernel(second, *refs)

    whole = pl.BlockSpec((WIDE, TERMS), lambda i, p: (0, 0))
    in_specs = [
        pl.BlockSpec((1, TILE, TERMS), lambda i, p: (p[0], i, 0)),
        pl.BlockSpec((1, 1, TILE), lambda i, p: (p[0], 0, i)),
        pl.BlockSpec((1, TERMS), lambda i, p: (0, 0)),
        whole,
        whole,
    ]
    args = [counts, row_idx, col_idx, row_pk, col_pk]
    if second:
        in_specs.append(whole)
        args.append(prev)
        row_shape = jax.ShapeDtypeStruct((2, WIDE, HALF), BF16)
        row_spec = pl.BlockSpec((2, WIDE, HALF), lambda i, p: (0, 0, 0))
    else:
        row_shape = jax.ShapeDtypeStruct((WIDE, TERMS), F32)
        row_spec = whole
    return pl.pallas_call(
        kernel,
        out_shape=(row_shape, jax.ShapeDtypeStruct((WIDE, TERMS), BF16)),
        grid_spec=pltpu.PrefetchScalarGridSpec(
            num_scalar_prefetch=1,
            grid=(TERMS // TILE,),
            in_specs=in_specs,
            out_specs=(row_spec, whole),
            scratch_shapes=[
                pltpu.VMEM((TERMS, TERMS), BF16),
                pltpu.VMEM((WIDE, TERMS), BF16),
                pltpu.VMEM((WIDE, TERMS), F32),
                pltpu.VMEM((WIDE, TERMS), F32),
            ],
        ),
        compiler_params=pltpu.CompilerParams(vmem_limit_bytes=40 * 2**20),
        cost_estimate=pl.CostEstimate(
            flops=7 * 2 * WIDE * TERMS * TERMS, bytes_accessed=8000000, transcendentals=3 * TERMS * TERMS
        ),
    )(pair, *args)


def adagrad_kernel(core_ref, mine_ref, other_ref, table_ref, acc_ref, out_ref):
    own = pl.program_id(0) == core_ref[0]
    total = jnp.where(own, mine_ref[...].astype(F32), other_ref[...].astype(F32))
    total = total.T[:, :DIM]
    step = LEARN_RATE * total * lax.rsqrt(acc_ref[...] + total * total)
    out_ref[...] = (table_ref[...].astype(F32) - step).astype(BF16)


def adagrad(core, mine, other, table, acc):
    half = pl.BlockSpec((WIDE, HALF), lambda i, c: (0, 0))
    part = pl.BlockSpec((HALF, DIM), lambda i, c: (i, 0))
    return pl.pallas_call(
        adagrad_kernel,
        out_shape=jax.ShapeDtypeStruct((TERMS, DIM), BF16),
        grid_spec=pltpu.PrefetchScalarGridSpec(
            num_scalar_prefetch=1,
            grid=(2,),
            in_specs=[half, half, part, part],
            out_specs=part,
        ),
        cost_estimate=pl.CostEstimate(flops=3000000, bytes_accessed=4000000, transcendentals=300000),
    )(core, mine, other, table, acc)


def add(*parts):
    total = parts[0].astype(F32)
    for part in parts[1:]:
        total = total + part.astype(F32)
    return total.astype(BF16)


def total_over_replicas(halves, core):
    keep = jnp.where(core == 0, halves[0], halves[1])
    give = jnp.where(core == 0, halves[1], halves[0])
    chip = add(keep, hop(give, CORE))
    mine = add(chip, hop(chip, ACROSS))
    return mine, hop(mine, CORE)


def per_device(
    row_emb, col_emb, row_acc, col_acc, row_offset, col_offset, counts, row_index, col_index
):
    replica = lax.axis_index("rep")
    core = replica & 1
    core_arg = core.reshape(1).astype(jnp.int32)
    first = (replica == 3).astype(jnp.int32)
    counts = counts.reshape(counts.shape[2:])
    row_idx = row_index.reshape(2, 1, TERMS)
    col_idx = col_index.reshape(2, 1, TERMS)
    swap = replica == 3
    give_1 = jnp.where(swap, col_idx[1], col_idx[0])
    give_2 = jnp.where(swap, col_idx[0], col_idx[1])
    idx_1 = hop(give_1, [(0, 0), (-1, 1), (-2, 2), (1, 3)])
    idx_2 = hop(give_2, [(-4, 0), (3, 1), (2, 2), (-3, 3)])

    col_pk = pack(col_emb, col_offset.reshape(1, TERMS), DIM, DIM + 1)
    got_1 = hop(col_pk, [(0, 0), (-1, 1), (-2, 2), (1, 3)])
    got_2 = hop(col_pk, [None, (3, 1), (2, 2), None])
    row_pk = pack(row_emb, row_offset.reshape(1, TERMS), DIM + 1, DIM)
    relayed = hop(got_1, [None, (-3, 0), (-1, 3), None])
    row_1, col_1 = score(first.reshape(1), counts, row_idx, idx_1, row_pk, got_1)
    block_2 = jnp.where((replica == 0) | swap, relayed, got_2)
    row_2, col_2 = score((1 - first).reshape(1), counts, row_idx, idx_2, row_pk, block_2, row_1)

    back_early = hop(col_1, [(0, 0), None, None, (-1, 3)])
    back_relay = hop(col_2, [(3, 1), None, None, (1, 2)])
    back_far = hop(col_2, [None, (-3, 0), (-2, 3), None])
    joined = add(col_1, back_relay)
    back_joined = hop(joined, [None, (1, 1), (2, 2), None])

    row_mine, row_other = total_over_replicas(row_2, core)
    new_row = adagrad(core_arg, row_mine, row_other, row_emb, row_acc)

    col_sum = add(back_early, back_far, back_joined)
    col_halves = jnp.stack([col_sum[:, :HALF], col_sum[:, HALF:]])
    col_mine, col_other = total_over_replicas(col_halves, core)
    new_col = adagrad(core_arg, col_mine, col_other, col_emb, col_acc)
    return (new_row, new_col)


def solution(mesh):
    in_specs = (
        P("blk", None),
        P("blk", None),
        P("blk", None),
        P("blk", None),
        P("blk"),
        P("blk"),
        P("blk", "rep", None, None, None),
        P("blk", "rep", None, None),
        P("blk", "rep", None, None),
    )
    out_specs = (P("blk", None), P("blk", None))
    return jax.shard_map(
        per_device, mesh=mesh, in_specs=in_specs, out_specs=out_specs, check_vma=False
    )
```

```python
import jax
import jax.numpy as jnp
from jax import lax
from jax.experimental import pallas as pl
from jax.experimental.pallas import tpu as pltpu
from jax.sharding import PartitionSpec as P

LEARN_RATE = 0.05
DIM = 300
WIDE = 304
LOW = 160
HIGH = WIDE - LOW
FULL = DIM // 16 * 16
OFF = DIM
ONE = DIM + 1
DIGIT = 32
TERMS = 1024
CHUNK = 256
RING = 8
STRIDE = 8
AXES = ("blk", "rep")
F32 = jnp.float32
BF16 = jnp.bfloat16


def hop(name, array, moves):
    perm = []
    for blk in range(RING * STRIDE):
        for rep in range(4):
            if moves[rep] is None:
                continue
            by, to = moves[rep]
            dst = (blk + STRIDE * by) % (RING * STRIDE)
            perm.append((blk * 4 + rep, dst * 4 + to))
    with jax.named_scope(name):
        return lax.ppermute(array, AXES, perm)


CORE = [(0, 1), (0, 0), (0, 3), (0, 2)]
ACROSS = [(0, 2), (0, 3), (0, 0), (0, 1)]


def dot(a, b, ca, cb):
    return lax.dot_general(a, b, (((ca,), (cb,)), ((), ())), preferred_element_type=F32)


def one_hot(index):
    hit = lax.broadcasted_iota(jnp.int32, (TERMS, TERMS), 0) == index
    return jnp.where(hit, 1.0, 0.0).astype(BF16)


def shape(rows, dtype=BF16):
    return jax.ShapeDtypeStruct((rows, TERMS), dtype)


def vmem(rows, dtype=BF16):
    return pltpu.VMEM((rows, TERMS), dtype)


def cost(flops, moved, trans=0):
    return pl.CostEstimate(flops=flops, bytes_accessed=moved, transcendentals=trans)


MATMUL = 2 * WIDE * TERMS * TERMS


def last_rows(emb_ref, tail, rows):
    left = DIM - FULL
    tail[:left] = emb_ref[FULL:DIM].astype(F32)
    for i, row in enumerate(rows):
        tail[left + i : left + i + 1] = row
    return tail[...].astype(BF16)


def order(ref, swap):
    idx = ref[...].reshape(2, TERMS)
    one, two = idx[:1], idx[1:]
    return jnp.where(swap, two, one), jnp.where(swap, one, two)


def pack_kernel(swap_ref, emb_ref, off_ref, idx_ref, low_ref, high_ref, idx_out, tail):
    idx, idx_2 = order(idx_ref, swap_ref[0] == 1)
    idx_out[...] = idx_2
    zero = jnp.zeros((1, TERMS), F32)
    high = (idx // DIGIT).astype(F32)
    low = (idx % DIGIT).astype(F32)
    off = off_ref[...].astype(F32).reshape(1, TERMS)
    low_ref[...] = emb_ref[:LOW]
    high_ref[: FULL - LOW] = emb_ref[LOW:FULL]
    high_ref[FULL - LOW :] = last_rows(emb_ref, tail, [off, high, low, zero])


KERNEL_VMEM = 20 * 2**20
VMEM = pl.BlockSpec(memory_space=pltpu.VMEM)
SMEM = pl.BlockSpec(memory_space=pltpu.SMEM)
HBM = pl.BlockSpec(memory_space=pltpu.HBM)


def pack(swap, emb, off, idx):
    return pl.pallas_call(
        pack_kernel,
        out_shape=(shape(LOW), shape(HIGH), shape(1, jnp.int32)),
        in_specs=[SMEM] + [VMEM] * 3,
        out_specs=(VMEM,) * 3,
        scratch_shapes=[pltpu.VMEM((16, TERMS), F32)],
        cost_estimate=cost(0, 1300000),
    )(swap, emb, off, idx)


def rows_kernel(swap_ref, emb_ref, off_ref, idx_ref, row_1, row_2, wide, tail):
    zero = jnp.zeros((1, TERMS), F32)
    off = off_ref[...].astype(F32).reshape(1, TERMS)
    wide[:FULL] = emb_ref[:FULL]
    wide[FULL:] = last_rows(emb_ref, tail, [zero + 1.0, off, zero, zero])
    for idx, out in zip(order(idx_ref, swap_ref[0] == 1), (row_1, row_2)):
        out[...] = dot(wide[...], one_hot(idx), 1, 0).astype(BF16)


def pick_rows(swap, emb, off, idx):
    return pl.pallas_call(
        rows_kernel,
        out_shape=(shape(WIDE), shape(WIDE)),
        in_specs=[SMEM] + [VMEM] * 3,
        out_specs=(VMEM,) * 2,
        scratch_shapes=[pltpu.VMEM((WIDE, TERMS), BF16), pltpu.VMEM((16, TERMS), F32)],
        cost_estimate=cost(2 * MATMUL, 2000000),
    )(swap, emb, off, idx)


def weights(count):
    scale = 1.0 / TERMS
    count_f = count.astype(F32)
    slope = 0.1 * scale + (0.25 * scale) * (count_f * lax.rsqrt(count_f))
    base = slope * jnp.log(count_f)
    return jnp.where(count > 0, slope, 0.0), jnp.where(count > 0, base, 0.0)


def cells(score, slope, base):
    scale = 0.5 / TERMS
    unseen = scale + scale * jnp.tanh(0.5 * score)
    return jnp.where(slope > 0, slope * score - base, unseen).astype(BF16)


CHUNKS = [slice(i, i + CHUNK) for i in range(0, TERMS, CHUNK)]


def fetch(pairs, sems):
    copies = [
        pltpu.make_async_copy(src, dst, sems.at[i]) for i, (src, dst) in enumerate(pairs)
    ]
    for copy in copies:
        copy.start()
    return copies


def pick_cols(block, pick):
    col = dot(block, pick, 1, 0)
    row = lax.broadcasted_iota(jnp.int32, (WIDE, TERMS), 0)
    return jnp.where(row > OFF, jnp.where(row == ONE, 1.0, 0.0), col).astype(BF16)


def put_halves(value, low_out, high_out):
    low_out[...] = value[:LOW]
    high_out[:HIGH] = value[LOW:]
    high_out[HIGH:] = jnp.zeros((LOW - HIGH, TERMS), BF16)


def first_kernel(
    swap_ref, counts_ref, row_ref, row_idx_ref, low_ref, high_ref, low_out, high_out, row_out,
    counts, cell_buf, row, sems,
):
    swap = swap_ref[0]
    at = [pl.ds(part.start, CHUNK) for part in CHUNKS]
    copies = fetch(
        [(row_ref, row)] + [(counts_ref.at[swap, part], counts.at[part]) for part in at], sems
    )
    digits = high_ref[HIGH - 16 :].astype(F32)
    one = ONE - (WIDE - 16)
    idx = (digits[one : one + 1] * DIGIT + digits[one + 1 : one + 2]).astype(jnp.int32)
    pick = one_hot(idx)
    col = pick_cols(jnp.concatenate([low_ref[...], high_ref[...]], axis=0), pick)
    copies[0].wait()
    for copy, part in zip(copies[1:], CHUNKS):
        score = dot(row[:, part], col, 0, 0)
        copy.wait()
        cell_buf[part] = cells(score, *weights(counts[part]))
    grad = dot(row[...], cell_buf[...], 1, 0).astype(BF16)
    put_halves(dot(grad, pick, 1, 1).astype(BF16), low_out, high_out)
    row_pick = one_hot(order(row_idx_ref, swap == 1)[0])
    row_out[...] = dot(dot(col, cell_buf[...], 1, 1).astype(BF16), row_pick, 1, 1)


def first_pair(swap, *args):
    return pl.pallas_call(
        first_kernel,
        out_shape=(shape(LOW), shape(LOW), shape(WIDE, F32)),
        in_specs=[SMEM, HBM, HBM] + [VMEM] * 3,
        out_specs=(VMEM,) * 3,
        scratch_shapes=[
            pltpu.VMEM((TERMS, TERMS), jnp.int32),
            pltpu.VMEM((TERMS, TERMS), BF16),
            pltpu.VMEM((WIDE, TERMS), BF16),
            pltpu.SemaphoreType.DMA((1 + len(CHUNKS),)),
        ],
        compiler_params=pltpu.CompilerParams(vmem_limit_bytes=KERNEL_VMEM),
        cost_estimate=cost(6 * MATMUL, 12000000, 3 * TERMS * TERMS),
    )(swap, *args)


def weigh_kernel(swap_ref, counts_ref, out_ref, buf, sems):
    at = [pl.ds(part.start, CHUNK) for part in CHUNKS]
    copies = fetch([(counts_ref.at[1 - swap_ref[0], part], buf.at[part]) for part in at], sems)
    for copy, part in zip(copies, CHUNKS):
        copy.wait()
        slope, base = weights(buf[part])
        out_ref[0, part] = slope.astype(BF16)
        out_ref[1, part] = base.astype(BF16)


def weigh(swap, counts):
    return pl.pallas_call(
        weigh_kernel,
        out_shape=jax.ShapeDtypeStruct((2, TERMS, TERMS), BF16),
        in_specs=[SMEM, HBM],
        out_specs=VMEM,
        scratch_shapes=[
            pltpu.VMEM((TERMS, TERMS), jnp.int32),
            pltpu.SemaphoreType.DMA((len(CHUNKS),)),
        ],
        compiler_params=pltpu.CompilerParams(vmem_limit_bytes=KERNEL_VMEM),
        cost_estimate=cost(20 * TERMS * TERMS, 8000000, 4 * TERMS * TERMS),
    )(swap, counts)


def second_kernel(
    swap_ref, weights_ref, row_ref, prev_ref, row_idx_ref, idx_ref, low_ref, high_ref, low_2_ref,
    high_2_ref, low_out, high_out, row_low_out, row_high_out, weight, cell_buf, row, prev, sems,
):
    at = [pl.ds(part.start, CHUNK) for part in CHUNKS]
    copies = fetch(
        [(row_ref, row)]
        + [(weights_ref.at[:, part], weight.at[:, part]) for part in at]
        + [(prev_ref, prev)],
        sems,
    )
    low = low_ref[...] + low_2_ref[...]
    high = high_ref[...] + high_2_ref[...]
    pick = one_hot(idx_ref[...])
    col = pick_cols(jnp.concatenate([low, high], axis=0), pick)
    copies[0].wait()
    for copy, part in zip(copies[1:-1], CHUNKS):
        score = dot(row[:, part], col, 0, 0)
        copy.wait()
        slope, base = weight[0, part].astype(F32), weight[1, part].astype(F32)
        cell_buf[part] = cells(score, slope, base)
    grad = dot(row[...], cell_buf[...], 1, 0).astype(BF16)
    put_halves(dot(grad, pick, 1, 1).astype(BF16), low_out, high_out)
    row_pick = one_hot(order(row_idx_ref, swap_ref[0] == 1)[1])
    total = dot(dot(col, cell_buf[...], 1, 1).astype(BF16), row_pick, 1, 1)
    copies[-1].wait()
    put_halves((prev[...] + total).astype(BF16), row_low_out, row_high_out)


def second_pair(swap, *args):
    return pl.pallas_call(
        second_kernel,
        out_shape=(vmem(LOW), vmem(LOW), shape(LOW), shape(LOW)),
        in_specs=[SMEM] + [HBM] * 3 + [VMEM] * 6,
        out_specs=(VMEM,) * 4,
        scratch_shapes=[
            pltpu.VMEM((2, TERMS, TERMS), BF16),
            pltpu.VMEM((TERMS, TERMS), BF16),
            pltpu.VMEM((WIDE, TERMS), BF16),
            pltpu.VMEM((WIDE, TERMS), F32),
            pltpu.SemaphoreType.DMA((2 + len(CHUNKS),)),
        ],
        compiler_params=pltpu.CompilerParams(vmem_limit_bytes=KERNEL_VMEM),
        cost_estimate=cost(6 * MATMUL, 12000000, TERMS * TERMS),
    )(swap, *args)


def adagrad(core, mine, other, table, acc):
    low = jnp.where(core == 0, mine, other)
    high = jnp.where(core == 0, other, mine)[: DIM - LOW]
    total = jnp.concatenate([low, high]).astype(F32)
    step = LEARN_RATE * total * lax.rsqrt(acc + total * total)
    return (table.astype(F32) - step).astype(BF16)


def in_hbm(array):
    return pltpu.with_memory_space_constraint(array, pltpu.HBM)


def add(*parts):
    total = parts[0].astype(F32)
    for part in parts[1:]:
        total = total + part.astype(F32)
    return total.astype(BF16)


def per_device(
    row_emb, col_emb, row_acc, col_acc, row_offset, col_offset, counts, row_index, col_index
):
    replica = lax.axis_index("rep")
    core = replica & 1
    is_0, is_1, is_3 = replica == 0, replica == 1, replica == 3
    swap = is_3.astype(jnp.int32).reshape(1)
    counts = in_hbm(counts.reshape(counts.shape[2:]))

    barrier = lax.optimization_barrier
    low, high, col_idx_2 = pack(swap, col_emb.T, col_offset, col_index)
    got_low = hop("got_low", low, [(0, 0), (-1, 1), (-2, 2), (1, 3)])
    far = hop("far", low, [None, (3, 1), None, None])
    got_high = hop("got_high", high, [(0, 0), (-1, 1), (-2, 2), (1, 3)])
    idx_2 = hop("idx_2", col_idx_2, [(-4, 0), (3, 1), (2, 2), (-3, 3)])
    row_1, row_2 = pick_rows(swap, row_emb.T, row_offset, row_index)
    weights_2 = weigh(swap, counts)
    got_low, got_high, far, idx_2, row_1, weights_2 = barrier(
        (got_low, got_high, far, idx_2, row_1, weights_2)
    )
    high_2 = hop("high_2", got_high, [None, (-3, 0), (-1, 3), (1, 2)])
    low_2 = hop("low_2", jnp.where(is_1, far, got_low), [None, (1, 0), (-1, 3), (1, 2)])
    low_1, high_1, row_sum = first_pair(
        swap, counts, in_hbm(row_1), row_index, got_low, got_high
    )
    high_2, low_2, low_1 = barrier((high_2, low_2, low_1))
    high_far = hop("high_far", high_2, [(-1, 1), None, None, None])
    give_low, give_high, row_low, row_high = second_pair(
        swap, in_hbm(weights_2), in_hbm(row_2), in_hbm(row_sum),
        row_index, idx_2, far, high_far, low_2, high_2,
    )

    s_low = hop("s_low", give_low, [(-1, 1), None, (-1, 3), (1, 2)])
    s_high = jnp.where(is_0, high_1, give_high)
    s_high = hop("s_high", s_high, [(0, 1), (1, 0), (-1, 3), (1, 2)])
    keep = jnp.where(core == 0, row_low, row_high)
    give = jnp.where(core == 0, row_high, row_low)
    row_chip = add(keep, hop("row_swap", give, CORE))
    s_low, s_high, row_chip = barrier((s_low, s_high, row_chip))
    one = jnp.where(is_0, give_high, jnp.where(is_1, give_low, jnp.where(is_3, high_1, low_1)))
    one = add(one, jnp.where(is_0 | is_3, s_high, s_low))
    one = hop("one", one, [(3, 1), (-3, 0), (2, 2), (-1, 3)])
    two = jnp.where(replica == 2, add(high_1, s_high), add(low_1, jnp.where(is_3, s_low, 0)))
    two = hop("two", two, [None, (1, 0), (2, 3), (-1, 2)])
    row_across = hop("row_across", row_chip, ACROSS)
    one, two = barrier((one, two))
    last = hop("last", add(high_1, one), [None, (1, 1), None, None])

    row_mine = add(row_chip, row_across)
    row_other = hop("row_other", row_mine, CORE)
    col_chip = add(
        jnp.where(is_1, s_high, one),
        jnp.where(is_1, last, two),
        jnp.where(is_0, low_1, 0),
    )
    col_across = hop("col_across", col_chip, ACROSS)
    new_row = adagrad(core, row_mine, row_other, row_emb.T, row_acc.T)
    col_across, new_row = barrier((col_across, new_row))
    col_mine = add(col_chip, col_across)
    col_other = hop("col_other", col_mine, CORE)
    new_col = adagrad(core, col_mine, col_other, col_emb.T, col_acc.T)
    return (new_row.T, new_col.T)


def solution(mesh):
    in_specs = (
        P("blk", None),
        P("blk", None),
        P("blk", None),
        P("blk", None),
        P("blk"),
        P("blk"),
        P("blk", "rep", None, None, None),
        P("blk", "rep", None, None),
        P("blk", "rep", None, None),
    )
    out_specs = (P("blk", None), P("blk", None))
    return jax.shard_map(
        per_device, mesh=mesh, in_specs=in_specs, out_specs=out_specs, check_vma=False
    )
```

```python
import jax
import jax.numpy as jnp
from jax import lax
from jax.experimental import pallas as pl
from jax.experimental.pallas import tpu as pltpu
from jax.sharding import PartitionSpec as P

LEARN_RATE = 0.05
DIM = 300
WIDE = 304
LOW = 160
HIGH = WIDE - LOW
FULL = DIM // 16 * 16
OFF = DIM
ONE = DIM + 1
DIGIT = 32
TERMS = 1024
RING = 8
STRIDE = 8
AXES = ("blk", "rep")
F32 = jnp.float32
BF16 = jnp.bfloat16


def hop(name, array, moves):
    perm = []
    for blk in range(RING * STRIDE):
        for rep in range(4):
            if moves[rep] is None:
                continue
            by, to = moves[rep]
            dst = (blk + STRIDE * by) % (RING * STRIDE)
            perm.append((blk * 4 + rep, dst * 4 + to))
    with jax.named_scope(name):
        return lax.ppermute(array, AXES, perm)


CORE = [(0, 1), (0, 0), (0, 3), (0, 2)]
ACROSS = [(0, 2), (0, 3), (0, 0), (0, 1)]


def dot(a, b, ca, cb):
    return lax.dot_general(a, b, (((ca,), (cb,)), ((), ())), preferred_element_type=F32)


def one_hot(index):
    hit = lax.broadcasted_iota(jnp.int32, (TERMS, TERMS), 0) == index
    return jnp.where(hit, 1.0, 0.0).astype(BF16)


def shape(rows, dtype=BF16):
    return jax.ShapeDtypeStruct((rows, TERMS), dtype)


def vmem(rows, dtype=BF16):
    return pltpu.VMEM((rows, TERMS), dtype)


def cost(flops, moved, trans=0):
    return pl.CostEstimate(flops=flops, bytes_accessed=moved, transcendentals=trans)


MATMUL = 2 * WIDE * TERMS * TERMS


def last_rows(emb_ref, tail, rows):
    left = DIM - FULL
    tail[:left] = emb_ref[FULL:DIM].astype(F32)
    for i, row in enumerate(rows):
        tail[left + i : left + i + 1] = row
    return tail[...].astype(BF16)


def order(ref, swap):
    idx = ref[...].reshape(2, TERMS)
    one, two = idx[:1], idx[1:]
    return jnp.where(swap, two, one), jnp.where(swap, one, two)


def pack_kernel(swap_ref, emb_ref, off_ref, idx_ref, out_ref, idx_out, tail):
    idx, idx_2 = order(idx_ref, swap_ref[0] == 1)
    idx_out[...] = idx_2
    zero = jnp.zeros((1, TERMS), F32)
    high = (idx // DIGIT).astype(F32)
    low = (idx % DIGIT).astype(F32)
    off = off_ref[...].astype(F32).reshape(1, TERMS)
    out_ref[:FULL] = emb_ref[:FULL]
    out_ref[FULL:] = last_rows(emb_ref, tail, [off, high, low, zero])


KERNEL_VMEM = 32 * 2**20
VMEM = pl.BlockSpec(memory_space=pltpu.VMEM)
SMEM = pl.BlockSpec(memory_space=pltpu.SMEM)
HBM = pl.BlockSpec(memory_space=pltpu.HBM)


def pack(swap, emb, off, idx):
    return pl.pallas_call(
        pack_kernel,
        out_shape=(shape(WIDE), shape(1, jnp.int32)),
        in_specs=[SMEM] + [VMEM] * 3,
        out_specs=(VMEM,) * 2,
        scratch_shapes=[pltpu.VMEM((16, TERMS), F32)],
        cost_estimate=cost(0, 1300000),
    )(swap, emb, off, idx)


def rows_kernel(swap_ref, emb_ref, off_ref, idx_ref, row_1, row_2, wide, tail):
    zero = jnp.zeros((1, TERMS), F32)
    off = off_ref[...].astype(F32).reshape(1, TERMS)
    wide[:FULL] = emb_ref[:FULL]
    wide[FULL:] = last_rows(emb_ref, tail, [zero + 1.0, off, zero, zero])
    for idx, out in zip(order(idx_ref, swap_ref[0] == 1), (row_1, row_2)):
        out[...] = dot(wide[...], one_hot(idx), 1, 0).astype(BF16)


def pick_rows(swap, emb, off, idx):
    return pl.pallas_call(
        rows_kernel,
        out_shape=(shape(WIDE), shape(WIDE)),
        in_specs=[SMEM] + [VMEM] * 3,
        out_specs=(VMEM,) * 2,
        scratch_shapes=[pltpu.VMEM((WIDE, TERMS), BF16), pltpu.VMEM((16, TERMS), F32)],
        cost_estimate=cost(2 * MATMUL, 2000000),
    )(swap, emb, off, idx)


def weights(count):
    scale = 1.0 / TERMS
    count_f = count.astype(F32)
    slope = 0.1 * scale + (0.25 * scale) * (count_f * lax.rsqrt(count_f))
    base = slope * jnp.log(count_f)
    return jnp.where(count > 0, slope, 0.0), jnp.where(count > 0, base, 0.0)


def cells(score, slope, base):
    scale = 0.5 / TERMS
    unseen = scale + scale * jnp.tanh(0.5 * score)
    return jnp.where(slope > 0, slope * score - base, unseen).astype(BF16)


def start(src, dst, sem):
    copy = pltpu.make_async_copy(src, dst, sem)
    copy.start()
    return copy


def score(pair, idx, block, counts_ref, row_ref, row_idx, counts, row, cell_buf, sems):
    get_row = start(row_ref, row, sems.at[0])
    get_counts = start(counts_ref.at[pair], counts, sems.at[1])
    pick = one_hot(idx)
    col = dot(block, pick, 1, 0)
    at = lax.broadcasted_iota(jnp.int32, (WIDE, TERMS), 0)
    col = jnp.where(at > OFF, jnp.where(at == ONE, 1.0, 0.0), col).astype(BF16)
    get_row.wait()
    est = dot(row[...], col, 0, 0)
    get_counts.wait()
    cell_buf[...] = cells(est, *weights(counts[...]))
    grad = dot(row[...], cell_buf[...], 1, 0).astype(BF16)
    grad = dot(grad, pick, 1, 1).astype(BF16)
    row_part = dot(col, cell_buf[...], 1, 1).astype(BF16)
    return grad, dot(row_part, one_hot(row_idx), 1, 1)


SCORE_SCRATCH = [
    pltpu.VMEM((TERMS, TERMS), jnp.int32),
    pltpu.VMEM((WIDE, TERMS), BF16),
    pltpu.VMEM((TERMS, TERMS), BF16),
    pltpu.SemaphoreType.DMA((3,)),
    pltpu.VMEM((WIDE, TERMS), F32),
]


def first_kernel(
    swap_ref, counts_ref, row_ref, row_idx_ref, block_ref, col_out, row_out,
    counts, row, cell_buf, sems, total,
):
    swap = swap_ref[0]
    digits = block_ref[FULL:].astype(F32)
    one = ONE - FULL
    idx = (digits[one : one + 1] * DIGIT + digits[one + 1 : one + 2]).astype(jnp.int32)
    row_idx = order(row_idx_ref, swap == 1)[0]
    grad, total[...] = score(
        swap, idx, block_ref[...], counts_ref, row_ref, row_idx, counts, row, cell_buf, sems
    )
    put = start(total, row_out, sems.at[2])
    col_out[...] = grad
    put.wait()


def first_pair(swap, *args):
    return pl.pallas_call(
        first_kernel,
        out_shape=(vmem(WIDE), pltpu.HBM((WIDE, TERMS), F32)),
        in_specs=[SMEM, HBM, HBM, VMEM, VMEM],
        out_specs=(VMEM, HBM),
        scratch_shapes=SCORE_SCRATCH,
        compiler_params=pltpu.CompilerParams(vmem_limit_bytes=KERNEL_VMEM),
        cost_estimate=cost(6 * MATMUL, 12000000, 3 * TERMS * TERMS),
    )(swap, *args)


def put_halves(value, low_out, high_out):
    low_out[...] = value[:LOW]
    high_out[:HIGH] = value[LOW:]
    high_out[HIGH:] = jnp.zeros((LOW - HIGH, TERMS), BF16)


def second_kernel(
    swap_ref, counts_ref, row_ref, prev_ref, row_idx_ref, idx_ref, block_ref, block_2_ref,
    low_out, high_out, row_low_out, row_high_out, counts, row, cell_buf, sems, prev,
):
    swap = swap_ref[0]
    get_prev = start(prev_ref, prev, sems.at[2])
    row_idx = order(row_idx_ref, swap == 1)[1]
    block = block_ref[...] + block_2_ref[...]
    grad, total = score(
        1 - swap, idx_ref[...], block, counts_ref, row_ref, row_idx, counts, row, cell_buf, sems
    )
    low_out[...] = grad[:LOW]
    high_out[...] = grad[LOW:]
    get_prev.wait()
    put_halves((prev[...] + total).astype(BF16), row_low_out, row_high_out)


def second_pair(swap, *args):
    return pl.pallas_call(
        second_kernel,
        out_shape=(vmem(LOW), vmem(HIGH), shape(LOW), shape(LOW)),
        in_specs=[SMEM] + [HBM] * 3 + [VMEM] * 4,
        out_specs=(VMEM,) * 4,
        scratch_shapes=SCORE_SCRATCH,
        compiler_params=pltpu.CompilerParams(vmem_limit_bytes=KERNEL_VMEM),
        cost_estimate=cost(6 * MATMUL, 12000000, 3 * TERMS * TERMS),
    )(swap, *args)


def adagrad(core, mine, other, table, acc):
    low = jnp.where(core == 0, mine, other)
    high = jnp.where(core == 0, other, mine)[: DIM - LOW]
    total = jnp.concatenate([low, high]).astype(F32)
    step = LEARN_RATE * total * lax.rsqrt(acc + total * total)
    return (table.astype(F32) - step).astype(BF16)


def in_hbm(array):
    return pltpu.with_memory_space_constraint(array, pltpu.HBM)


def halves(core, low, high):
    return jnp.where(core == 0, low, high), jnp.where(core == 0, high, low)


def add(*parts):
    total = parts[0].astype(F32)
    for part in parts[1:]:
        total = total + part.astype(F32)
    return total.astype(BF16)


def per_device(
    row_emb, col_emb, row_acc, col_acc, row_offset, col_offset, counts, row_index, col_index
):
    replica = lax.axis_index("rep")
    core = replica & 1
    is_0, is_3 = replica == 0, replica == 3
    swap = is_3.astype(jnp.int32).reshape(1)
    counts = in_hbm(counts.reshape(counts.shape[2:]))

    barrier = lax.optimization_barrier
    block, col_idx_2 = pack(swap, col_emb.T, col_offset, col_index)
    got = hop("got", block, [(0, 0), (-1, 1), (-2, 2), (1, 3)])
    far = hop("far", block, [None, (3, 1), None, None])
    idx_2 = hop("idx_2", col_idx_2, [(-4, 0), (3, 1), (2, 2), (-3, 3)])
    row_1, row_2 = pick_rows(swap, row_emb.T, row_offset, row_index)
    got, row_1 = barrier((got, row_1))
    near = hop("near", got, [None, (-3, 0), (-1, 3), (1, 2)])
    grad_1, row_sum = first_pair(swap, counts, in_hbm(row_1), row_index, got)
    near, far, idx_2, grad_1 = barrier((near, far, idx_2, grad_1))
    low, high, row_low, row_high = second_pair(
        swap, counts, in_hbm(row_2), in_hbm(row_sum), row_index, idx_2, far, near
    )

    way = [(3, 1), (-3, 0), (-1, 3), (1, 2)]
    low = hop("low", low, way)
    high = hop("high", high, way)
    row_keep, row_give = halves(core, row_low, row_high)
    row_chip = add(row_keep, hop("row_swap", row_give, CORE))
    low, row_chip = barrier((low, row_chip))
    low = add(grad_1[:LOW], low)
    low_up = hop("low_up", low, [None, (1, 0), (2, 2), None])
    low_down = hop("low_down", low, [None, None, None, (-1, 2)])
    high = add(grad_1[LOW:], high)
    high_up = hop("high_up", high, [None, (1, 1), (2, 3), None])
    high_down = hop("high_down", high, [(0, 1), None, None, (-1, 3)])
    low = add(low_up, low_down, jnp.where(is_0, low, 0))
    high = jnp.pad(add(high_up, high_down), ((0, LOW - HIGH), (0, 0)))
    col_chip = halves(core, low, high)[0]
    col_across = hop("col_across", col_chip, ACROSS)
    row_across = hop("row_across", row_chip, ACROSS)
    col_across, row_across = barrier((col_across, row_across))
    row_mine = add(row_chip, row_across)
    row_other = hop("row_other", row_mine, CORE)
    new_row = adagrad(core, row_mine, row_other, row_emb.T, row_acc.T)
    col_mine = add(col_chip, col_across)
    col_other = hop("col_other", col_mine, CORE)
    new_col = adagrad(core, col_mine, col_other, col_emb.T, col_acc.T)
    return (new_row.T, new_col.T)


def solution(mesh):
    in_specs = (
        P("blk", None),
        P("blk", None),
        P("blk", None),
        P("blk", None),
        P("blk"),
        P("blk"),
        P("blk", "rep", None, None, None),
        P("blk", "rep", None, None),
        P("blk", "rep", None, None),
    )
    out_specs = (P("blk", None), P("blk", None))
    return jax.shard_map(
        per_device, mesh=mesh, in_specs=in_specs, out_specs=out_specs, check_vma=False
    )
```

```python
import jax
import jax.numpy as jnp
from jax import lax
from jax.experimental import pallas as pl
from jax.experimental.pallas import tpu as pltpu
from jax.sharding import PartitionSpec as P

LEARN_RATE = 0.05
DIM = 300
WIDE = 304
LOW = 160
HIGH = WIDE - LOW
FULL = DIM // 16 * 16
OFF = DIM
ONE = DIM + 1
DIGIT = 32
TERMS = 1024
RING = 8
STRIDE = 8
AXES = ("blk", "rep")
F32 = jnp.float32
BF16 = jnp.bfloat16


def hop(name, array, moves):
    perm = []
    for blk in range(RING * STRIDE):
        for rep in range(4):
            if moves[rep] is None:
                continue
            by, to = moves[rep]
            dst = (blk + STRIDE * by) % (RING * STRIDE)
            perm.append((blk * 4 + rep, dst * 4 + to))
    with jax.named_scope(name):
        return lax.ppermute(array, AXES, perm)


CORE = [(0, 1), (0, 0), (0, 3), (0, 2)]
ACROSS = [(0, 2), (0, 3), (0, 0), (0, 1)]


def dot(a, b, ca, cb):
    return lax.dot_general(a, b, (((ca,), (cb,)), ((), ())), preferred_element_type=F32)


def one_hot(index):
    hit = lax.broadcasted_iota(jnp.int32, (TERMS, TERMS), 0) == index
    return jnp.where(hit, 1.0, 0.0).astype(BF16)


def shape(rows, dtype=BF16):
    return jax.ShapeDtypeStruct((rows, TERMS), dtype)


def vmem(rows, dtype=BF16):
    return pltpu.VMEM((rows, TERMS), dtype)


def cost(flops, moved, trans=0):
    return pl.CostEstimate(flops=flops, bytes_accessed=moved, transcendentals=trans)


MATMUL = 2 * WIDE * TERMS * TERMS


def last_rows(emb_ref, tail, rows):
    left = DIM - FULL
    tail[:left] = emb_ref[FULL:DIM].astype(F32)
    for i, row in enumerate(rows):
        tail[left + i : left + i + 1] = row
    return tail[...].astype(BF16)


def order(ref, swap):
    idx = ref[...].reshape(2, TERMS)
    one, two = idx[:1], idx[1:]
    return jnp.where(swap, two, one), jnp.where(swap, one, two)


def pack_kernel(swap_ref, emb_ref, off_ref, idx_ref, out_ref, idx_out, tail):
    idx, idx_2 = order(idx_ref, swap_ref[0] == 1)
    idx_out[...] = idx_2
    zero = jnp.zeros((1, TERMS), F32)
    high = (idx // DIGIT).astype(F32)
    low = (idx % DIGIT).astype(F32)
    off = off_ref[...].astype(F32).reshape(1, TERMS)
    out_ref[:FULL] = emb_ref[:FULL]
    out_ref[FULL:] = last_rows(emb_ref, tail, [off, high, low, zero])


KERNEL_VMEM = 32 * 2**20
VMEM = pl.BlockSpec(memory_space=pltpu.VMEM)
SMEM = pl.BlockSpec(memory_space=pltpu.SMEM)
HBM = pl.BlockSpec(memory_space=pltpu.HBM)


def pack(swap, emb, off, idx):
    return pl.pallas_call(
        pack_kernel,
        out_shape=(shape(WIDE), shape(1, jnp.int32)),
        in_specs=[SMEM] + [VMEM] * 3,
        out_specs=(VMEM,) * 2,
        scratch_shapes=[pltpu.VMEM((16, TERMS), F32)],
        cost_estimate=cost(0, 1300000),
    )(swap, emb, off, idx)


def rows_kernel(swap_ref, emb_ref, off_ref, idx_ref, row_1, row_2, wide, tail):
    zero = jnp.zeros((1, TERMS), F32)
    off = off_ref[...].astype(F32).reshape(1, TERMS)
    wide[:FULL] = emb_ref[:FULL]
    wide[FULL:] = last_rows(emb_ref, tail, [zero + 1.0, off, zero, zero])
    for idx, out in zip(order(idx_ref, swap_ref[0] == 1), (row_1, row_2)):
        out[...] = dot(wide[...], one_hot(idx), 1, 0).astype(BF16)


def pick_rows(swap, emb, off, idx):
    return pl.pallas_call(
        rows_kernel,
        out_shape=(shape(WIDE), shape(WIDE)),
        in_specs=[SMEM] + [VMEM] * 3,
        out_specs=(VMEM,) * 2,
        scratch_shapes=[pltpu.VMEM((WIDE, TERMS), BF16), pltpu.VMEM((16, TERMS), F32)],
        cost_estimate=cost(2 * MATMUL, 2000000),
    )(swap, emb, off, idx)


def weights(count):
    scale = 1.0 / TERMS
    count_f = count.astype(F32)
    slope = 0.1 * scale + (0.25 * scale) * (count_f * lax.rsqrt(count_f))
    base = slope * jnp.log(count_f)
    return jnp.where(count > 0, slope, 0.0), jnp.where(count > 0, base, 0.0)


def cells(score, slope, base):
    scale = 0.5 / TERMS
    unseen = scale + scale * jnp.tanh(0.5 * score)
    return jnp.where(slope > 0, slope * score - base, unseen).astype(BF16)


def start(src, dst, sem):
    copy = pltpu.make_async_copy(src, dst, sem)
    copy.start()
    return copy


def score(pair, idx, block, counts_ref, row_ref, row_idx, counts, row, cell_buf, sems):
    get_row = start(row_ref, row, sems.at[0])
    get_counts = start(counts_ref.at[pair], counts, sems.at[1])
    pick = one_hot(idx)
    col = dot(block, pick, 1, 0)
    at = lax.broadcasted_iota(jnp.int32, (WIDE, TERMS), 0)
    col = jnp.where(at > OFF, jnp.where(at == ONE, 1.0, 0.0), col).astype(BF16)
    get_row.wait()
    est = dot(row[...], col, 0, 0)
    get_counts.wait()
    cell_buf[...] = cells(est, *weights(counts[...]))
    grad = dot(row[...], cell_buf[...], 1, 0).astype(BF16)
    grad = dot(grad, pick, 1, 1).astype(BF16)
    row_part = dot(col, cell_buf[...], 1, 1).astype(BF16)
    return grad, dot(row_part, one_hot(row_idx), 1, 1)


SCORE_SCRATCH = [
    pltpu.VMEM((TERMS, TERMS), jnp.int32),
    pltpu.VMEM((WIDE, TERMS), BF16),
    pltpu.VMEM((TERMS, TERMS), BF16),
    pltpu.SemaphoreType.DMA((3,)),
    pltpu.VMEM((WIDE, TERMS), F32),
]


def first_kernel(
    swap_ref, counts_ref, row_ref, row_idx_ref, block_ref, col_out, row_out,
    counts, row, cell_buf, sems, total,
):
    swap = swap_ref[0]
    digits = block_ref[FULL:].astype(F32)
    one = ONE - FULL
    idx = (digits[one : one + 1] * DIGIT + digits[one + 1 : one + 2]).astype(jnp.int32)
    row_idx = order(row_idx_ref, swap == 1)[0]
    grad, total[...] = score(
        swap, idx, block_ref[...], counts_ref, row_ref, row_idx, counts, row, cell_buf, sems
    )
    put = start(total, row_out, sems.at[2])
    col_out[...] = grad
    put.wait()


def first_pair(swap, *args):
    return pl.pallas_call(
        first_kernel,
        out_shape=(vmem(WIDE), pltpu.HBM((WIDE, TERMS), F32)),
        in_specs=[SMEM, HBM, HBM, VMEM, VMEM],
        out_specs=(VMEM, HBM),
        scratch_shapes=SCORE_SCRATCH,
        compiler_params=pltpu.CompilerParams(vmem_limit_bytes=KERNEL_VMEM),
        cost_estimate=cost(6 * MATMUL, 12000000, 3 * TERMS * TERMS),
    )(swap, *args)


def put_halves(value, low_out, high_out):
    low_out[...] = value[:LOW]
    high_out[:HIGH] = value[LOW:]
    high_out[HIGH:] = jnp.zeros((LOW - HIGH, TERMS), BF16)


def second_kernel(
    swap_ref, counts_ref, row_ref, prev_ref, row_idx_ref, idx_ref, block_ref, block_2_ref,
    low_out, high_out, row_low_out, row_high_out, counts, row, cell_buf, sems, prev,
):
    swap = swap_ref[0]
    get_prev = start(prev_ref, prev, sems.at[2])
    row_idx = order(row_idx_ref, swap == 1)[1]
    block = block_ref[...] + block_2_ref[...]
    grad, total = score(
        1 - swap, idx_ref[...], block, counts_ref, row_ref, row_idx, counts, row, cell_buf, sems
    )
    low_out[...] = grad[:LOW]
    high_out[...] = grad[LOW:]
    get_prev.wait()
    put_halves((prev[...] + total).astype(BF16), row_low_out, row_high_out)


def second_pair(swap, *args):
    return pl.pallas_call(
        second_kernel,
        out_shape=(vmem(LOW), vmem(HIGH), shape(LOW), shape(LOW)),
        in_specs=[SMEM] + [HBM] * 3 + [VMEM] * 4,
        out_specs=(VMEM,) * 4,
        scratch_shapes=SCORE_SCRATCH,
        compiler_params=pltpu.CompilerParams(vmem_limit_bytes=KERNEL_VMEM),
        cost_estimate=cost(6 * MATMUL, 12000000, 3 * TERMS * TERMS),
    )(swap, *args)


def adagrad(low, high, table, acc):
    total = jnp.concatenate([low, high[: DIM - LOW]]).astype(F32)
    step = LEARN_RATE * total * lax.rsqrt(acc + total * total)
    return (table.astype(F32) - step).astype(BF16)


def in_hbm(array):
    return pltpu.with_memory_space_constraint(array, pltpu.HBM)


def halves(core, low, high):
    return jnp.where(core == 0, low, high), jnp.where(core == 0, high, low)


def add(*parts):
    total = parts[0].astype(F32)
    for part in parts[1:]:
        total = total + part.astype(F32)
    return total.astype(BF16)


def per_device(
    row_emb, col_emb, row_acc, col_acc, row_offset, col_offset, counts, row_index, col_index
):
    replica = lax.axis_index("rep")
    core = replica & 1
    is_0, is_3 = replica == 0, replica == 3
    swap = is_3.astype(jnp.int32).reshape(1)
    counts = in_hbm(counts.reshape(counts.shape[2:]))

    barrier = lax.optimization_barrier
    block, col_idx_2 = pack(swap, col_emb.T, col_offset, col_index)
    got = hop("got", block, [(0, 0), (-1, 1), (-2, 2), (1, 3)])
    far = hop("far", block, [None, (3, 1), None, None])
    idx_2 = hop("idx_2", col_idx_2, [(-4, 0), (3, 1), (2, 2), (-3, 3)])
    row_1, row_2 = pick_rows(swap, row_emb.T, row_offset, row_index)
    got, row_1 = barrier((got, row_1))
    near = hop("near", got, [None, (-3, 0), (-1, 3), (1, 2)])
    grad_1, row_sum = first_pair(swap, counts, in_hbm(row_1), row_index, got)
    near, far, idx_2, grad_1 = barrier((near, far, idx_2, grad_1))
    low, high, row_low, row_high = second_pair(
        swap, counts, in_hbm(row_2), in_hbm(row_sum), row_index, idx_2, far, near
    )

    way = [(3, 1), (-3, 0), (-1, 3), (1, 2)]
    low = hop("low", low, way)
    high = hop("high", high, way)
    row_keep, row_give = halves(core, row_low, row_high)
    row_chip = add(row_keep, hop("row_swap", row_give, CORE))
    row_across = hop("row_across", row_chip, ACROSS)
    high, row_across = barrier((add(grad_1[LOW:], high), row_across))
    low = add(grad_1[:LOW], low)
    low_up = hop("low_up", low, [None, (1, 0), (2, 2), None])
    low_down = hop("low_down", low, [None, None, None, (-1, 2)])
    high_up = hop("high_up", high, [None, (1, 0), (2, 3), None])
    high_down = hop("high_down", high, [None, None, None, (-1, 3)])
    high = add(high_up, high_down, jnp.where(is_0, high, 0))
    high_across = hop("high_across", high, [(0, 3), None, None, (0, 0)])
    high = add(high, high_across)
    high = high + hop("high_other", high, [(0, 1), None, None, (0, 2)])
    low_up, row_across = barrier((low_up, row_across))
    row_mine = add(row_chip, row_across)
    row_other = hop("row_other", row_mine, CORE)
    row_low, row_high = halves(core, row_mine, row_other)
    new_row = adagrad(row_low, row_high, row_emb.T, row_acc.T)

    low = add(low_up, low_down, jnp.where(is_0, low, 0))
    low_across = hop("low_across", low, [(0, 2), None, (0, 0), None])
    low_across, new_row = barrier((low_across, new_row))
    low = add(low, low_across)
    low = low + hop("low_other", low, [(0, 1), None, (0, 3), None])
    new_col = adagrad(low, high, col_emb.T, col_acc.T)
    return (new_row.T, new_col.T)


def solution(mesh):
    in_specs = (
        P("blk", None),
        P("blk", None),
        P("blk", None),
        P("blk", None),
        P("blk"),
        P("blk"),
        P("blk", "rep", None, None, None),
        P("blk", "rep", None, None),
        P("blk", "rep", None, None),
    )
    out_specs = (P("blk", None), P("blk", None))
    return jax.shard_map(
        per_device, mesh=mesh, in_specs=in_specs, out_specs=out_specs, check_vma=False
    )
```

```python
import jax
import jax.numpy as jnp
from jax import lax
from jax.experimental import pallas as pl
from jax.experimental.pallas import tpu as pltpu
from jax.sharding import PartitionSpec as P

LEARN_RATE = 0.05
DIM = 300
WIDE = 304
LOW = 160
HIGH = WIDE - LOW
FULL = DIM // 16 * 16
OFF = DIM
ONE = DIM + 1
DIGIT = 32
TERMS = 1024
RING = 8
STRIDE = 8
AXES = ("blk", "rep")
F32 = jnp.float32
BF16 = jnp.bfloat16


def hop(name, array, moves):
    perm = []
    for blk in range(RING * STRIDE):
        for rep in range(4):
            if moves[rep] is None:
                continue
            by, to = moves[rep]
            dst = (blk + STRIDE * by) % (RING * STRIDE)
            perm.append((blk * 4 + rep, dst * 4 + to))
    with jax.named_scope(name):
        return lax.ppermute(array, AXES, perm)


CORE = [(0, 1), (0, 0), (0, 3), (0, 2)]
ACROSS = [(0, 2), (0, 3), (0, 0), (0, 1)]


def dot(a, b, ca, cb):
    return lax.dot_general(a, b, (((ca,), (cb,)), ((), ())), preferred_element_type=F32)


def one_hot(index):
    hit = lax.broadcasted_iota(jnp.int32, (TERMS, TERMS), 0) == index
    return jnp.where(hit, 1.0, 0.0).astype(BF16)


def shape(rows, dtype=BF16):
    return jax.ShapeDtypeStruct((rows, TERMS), dtype)


def vmem(rows, dtype=BF16):
    return pltpu.VMEM((rows, TERMS), dtype)


def cost(flops, moved, trans=0):
    return pl.CostEstimate(flops=flops, bytes_accessed=moved, transcendentals=trans)


MATMUL = 2 * WIDE * TERMS * TERMS


def last_rows(emb_ref, tail, rows):
    left = DIM - FULL
    tail[:left] = emb_ref[FULL:DIM].astype(F32)
    for i, row in enumerate(rows):
        tail[left + i : left + i + 1] = row
    return tail[...].astype(BF16)


def order(ref, swap):
    idx = ref[...].reshape(2, TERMS)
    one, two = idx[:1], idx[1:]
    return jnp.where(swap, two, one), jnp.where(swap, one, two)


def pack_kernel(swap_ref, emb_ref, off_ref, idx_ref, out_ref, idx_out, tail):
    idx, idx_2 = order(idx_ref, swap_ref[0] == 1)
    idx_out[...] = idx_2
    zero = jnp.zeros((1, TERMS), F32)
    high = (idx // DIGIT).astype(F32)
    low = (idx % DIGIT).astype(F32)
    off = off_ref[...].astype(F32).reshape(1, TERMS)
    out_ref[:FULL] = emb_ref[:FULL]
    out_ref[FULL:] = last_rows(emb_ref, tail, [off, high, low, zero])


KERNEL_VMEM = 32 * 2**20
VMEM = pl.BlockSpec(memory_space=pltpu.VMEM)
SMEM = pl.BlockSpec(memory_space=pltpu.SMEM)
HBM = pl.BlockSpec(memory_space=pltpu.HBM)


def pack(swap, emb, off, idx):
    return pl.pallas_call(
        pack_kernel,
        out_shape=(shape(WIDE), shape(1, jnp.int32)),
        in_specs=[SMEM] + [VMEM] * 3,
        out_specs=(VMEM,) * 2,
        scratch_shapes=[pltpu.VMEM((16, TERMS), F32)],
        cost_estimate=cost(0, 1300000),
    )(swap, emb, off, idx)


def rows_kernel(swap_ref, emb_ref, off_ref, idx_ref, row_1, row_2, wide, tail):
    zero = jnp.zeros((1, TERMS), F32)
    off = off_ref[...].astype(F32).reshape(1, TERMS)
    wide[:FULL] = emb_ref[:FULL]
    wide[FULL:] = last_rows(emb_ref, tail, [zero + 1.0, off, zero, zero])
    for idx, out in zip(order(idx_ref, swap_ref[0] == 1), (row_1, row_2)):
        out[...] = dot(wide[...], one_hot(idx), 1, 0).astype(BF16)


def pick_rows(swap, emb, off, idx):
    return pl.pallas_call(
        rows_kernel,
        out_shape=(shape(WIDE), shape(WIDE)),
        in_specs=[SMEM] + [VMEM] * 3,
        out_specs=(VMEM,) * 2,
        scratch_shapes=[pltpu.VMEM((WIDE, TERMS), BF16), pltpu.VMEM((16, TERMS), F32)],
        cost_estimate=cost(2 * MATMUL, 2000000),
    )(swap, emb, off, idx)


def cells(score, count):
    scale = 1.0 / TERMS
    count_f = count.astype(F32)
    slope = 0.1 * scale + (0.25 * scale) * (count_f * lax.rsqrt(count_f))
    seen = slope * (score - jnp.log(count_f))
    unseen = 0.5 * scale + (0.5 * scale) * jnp.tanh(0.5 * score)
    return jnp.where(count > 0, seen, unseen).astype(BF16)


def start(src, dst, sem):
    copy = pltpu.make_async_copy(src, dst, sem)
    copy.start()
    return copy


def score(pair, idx, block, counts_ref, row_ref, row_idx, counts, row, cell_buf, sems):
    get_row = start(row_ref, row, sems.at[0])
    get_counts = start(counts_ref.at[pair], counts, sems.at[1])
    pick = one_hot(idx)
    col = dot(block, pick, 1, 0)
    at = lax.broadcasted_iota(jnp.int32, (WIDE, TERMS), 0)
    col = jnp.where(at > OFF, jnp.where(at == ONE, 1.0, 0.0), col).astype(BF16)
    get_row.wait()
    est = dot(row[...], col, 0, 0)
    get_counts.wait()
    cell_buf[...] = cells(est, counts[...])
    grad = dot(row[...], cell_buf[...], 1, 0).astype(BF16)
    grad = dot(grad, pick, 1, 1).astype(BF16)
    row_part = dot(col, cell_buf[...], 1, 1).astype(BF16)
    return grad, dot(row_part, one_hot(row_idx), 1, 1)


SCORE_SCRATCH = [
    pltpu.VMEM((TERMS, TERMS), jnp.int32),
    pltpu.VMEM((WIDE, TERMS), BF16),
    pltpu.VMEM((TERMS, TERMS), BF16),
    pltpu.SemaphoreType.DMA((3,)),
    pltpu.VMEM((WIDE, TERMS), F32),
]


def first_kernel(
    swap_ref, counts_ref, row_ref, row_idx_ref, block_ref, col_out, row_out,
    counts, row, cell_buf, sems, total,
):
    swap = swap_ref[0]
    digits = block_ref[FULL:].astype(F32)
    one = ONE - FULL
    idx = (digits[one : one + 1] * DIGIT + digits[one + 1 : one + 2]).astype(jnp.int32)
    row_idx = order(row_idx_ref, swap == 1)[0]
    grad, total[...] = score(
        swap, idx, block_ref[...], counts_ref, row_ref, row_idx, counts, row, cell_buf, sems
    )
    put = start(total, row_out, sems.at[2])
    col_out[...] = grad
    put.wait()


def first_pair(swap, *args):
    return pl.pallas_call(
        first_kernel,
        out_shape=(vmem(WIDE), pltpu.HBM((WIDE, TERMS), F32)),
        in_specs=[SMEM, HBM, HBM, VMEM, VMEM],
        out_specs=(VMEM, HBM),
        scratch_shapes=SCORE_SCRATCH,
        compiler_params=pltpu.CompilerParams(vmem_limit_bytes=KERNEL_VMEM),
        cost_estimate=cost(6 * MATMUL, 12000000, 3 * TERMS * TERMS),
    )(swap, *args)


def put_halves(value, low_out, high_out):
    low_out[...] = value[:LOW]
    high_out[:HIGH] = value[LOW:]
    high_out[HIGH:] = jnp.zeros((LOW - HIGH, TERMS), BF16)


def second_kernel(
    swap_ref, counts_ref, row_ref, prev_ref, row_idx_ref, idx_ref, block_ref, block_2_ref,
    low_out, high_out, row_low_out, row_high_out, counts, row, cell_buf, sems, prev,
):
    swap = swap_ref[0]
    get_prev = start(prev_ref, prev, sems.at[2])
    row_idx = order(row_idx_ref, swap == 1)[1]
    block = block_ref[...] + block_2_ref[...]
    grad, total = score(
        1 - swap, idx_ref[...], block, counts_ref, row_ref, row_idx, counts, row, cell_buf, sems
    )
    low_out[...] = grad[:LOW]
    high_out[...] = grad[LOW:]
    get_prev.wait()
    put_halves((prev[...] + total).astype(BF16), row_low_out, row_high_out)


def second_pair(swap, *args):
    return pl.pallas_call(
        second_kernel,
        out_shape=(vmem(LOW), vmem(HIGH), shape(LOW), shape(LOW)),
        in_specs=[SMEM] + [HBM] * 3 + [VMEM] * 4,
        out_specs=(VMEM,) * 4,
        scratch_shapes=SCORE_SCRATCH,
        compiler_params=pltpu.CompilerParams(vmem_limit_bytes=KERNEL_VMEM),
        cost_estimate=cost(6 * MATMUL, 12000000, 3 * TERMS * TERMS),
    )(swap, *args)


def adagrad(low, high, table, acc):
    total = jnp.concatenate([low, high[: DIM - LOW]]).astype(F32)
    step = LEARN_RATE * total * lax.rsqrt(acc + total * total)
    return (table.astype(F32) - step).astype(BF16)


def in_hbm(array):
    return pltpu.with_memory_space_constraint(array, pltpu.HBM)


def halves(core, low, high):
    return jnp.where(core == 0, low, high), jnp.where(core == 0, high, low)


def add(*parts):
    total = parts[0].astype(F32)
    for part in parts[1:]:
        total = total + part.astype(F32)
    return total.astype(BF16)


def per_device(
    row_emb, col_emb, row_acc, col_acc, row_offset, col_offset, counts, row_index, col_index
):
    replica = lax.axis_index("rep")
    core = replica & 1
    is_0, is_3 = replica == 0, replica == 3
    swap = is_3.astype(jnp.int32).reshape(1)
    counts = in_hbm(counts.reshape(counts.shape[2:]))

    barrier = lax.optimization_barrier
    block, col_idx_2 = pack(swap, col_emb.T, col_offset, col_index)
    got = hop("got", block, [(0, 0), (-1, 1), (-2, 2), (1, 3)])
    far = hop("far", block, [None, (3, 1), None, None])
    idx_2 = hop("idx_2", col_idx_2, [(-4, 0), (3, 1), (2, 2), (-3, 3)])
    row_1, row_2 = pick_rows(swap, row_emb.T, row_offset, row_index)
    got, row_1 = barrier((got, row_1))
    near = hop("near", got, [None, (-3, 0), (-1, 3), (1, 2)])
    grad_1, row_sum = first_pair(swap, counts, in_hbm(row_1), row_index, got)
    near, far, idx_2, grad_1 = barrier((near, far, idx_2, grad_1))
    low, high, row_low, row_high = second_pair(
        swap, counts, in_hbm(row_2), in_hbm(row_sum), row_index, idx_2, far, near
    )

    way = [(3, 1), (-3, 0), (-1, 3), (1, 2)]
    low = hop("low", low, way)
    high = hop("high", high, way)
    row_keep, row_give = halves(core, row_low, row_high)
    row_chip = add(row_keep, hop("row_swap", row_give, CORE))
    row_across = hop("row_across", row_chip, ACROSS)
    high, row_across = barrier((add(grad_1[LOW:], high), row_across))
    low = add(grad_1[:LOW], low)
    low_up = hop("low_up", low, [None, (1, 0), (2, 2), None])
    low_down = hop("low_down", low, [None, None, None, (-1, 2)])
    high_up = hop("high_up", high, [None, (1, 0), (2, 3), None])
    high_down = hop("high_down", high, [None, None, None, (-1, 3)])
    high = add(high_up, high_down, jnp.where(is_0, high, 0))
    high_across = hop("high_across", high, [(0, 3), None, None, (0, 0)])
    high = add(high, high_across)
    high = high + hop("high_other", high, [(0, 1), None, None, (0, 2)])
    low_up, row_across = barrier((low_up, row_across))
    row_mine = add(row_chip, row_across)
    row_other = hop("row_other", row_mine, CORE)
    row_low, row_high = halves(core, row_mine, row_other)
    new_row = adagrad(row_low, row_high, row_emb.T, row_acc.T)

    low = add(low_up, low_down, jnp.where(is_0, low, 0))
    low_across = hop("low_across", low, [(0, 2), None, (0, 0), None])
    low_across, new_row = barrier((low_across, new_row))
    low = add(low, low_across)
    low = low + hop("low_other", low, [(0, 1), None, (0, 3), None])
    new_col = adagrad(low, high, col_emb.T, col_acc.T)
    return (new_row.T, new_col.T)


def solution(mesh):
    in_specs = (
        P("blk", None),
        P("blk", None),
        P("blk", None),
        P("blk", None),
        P("blk"),
        P("blk"),
        P("blk", "rep", None, None, None),
        P("blk", "rep", None, None),
        P("blk", "rep", None, None),
    )
    out_specs = (P("blk", None), P("blk", None))
    return jax.shard_map(
        per_device, mesh=mesh, in_specs=in_specs, out_specs=out_specs, check_vma=False
    )
```

```python
import jax
import jax.numpy as jnp
from jax import lax
from jax.experimental import pallas as pl
from jax.experimental.pallas import tpu as pltpu
from jax.sharding import PartitionSpec as P

LEARN_RATE = 0.05
DIM = 300
WIDE = 304
LOW = 160
HIGH = WIDE - LOW
FULL = DIM // 16 * 16
OFF = DIM
ONE = DIM + 1
DIGIT = 32
TERMS = 1024
RING = 8
STRIDE = 8
AXES = ("blk", "rep")
F32 = jnp.float32
BF16 = jnp.bfloat16


def hop(name, array, moves):
    perm = []
    for blk in range(RING * STRIDE):
        for rep in range(4):
            if moves[rep] is None:
                continue
            by, to = moves[rep]
            dst = (blk + STRIDE * by) % (RING * STRIDE)
            perm.append((blk * 4 + rep, dst * 4 + to))
    with jax.named_scope(name):
        return lax.ppermute(array, AXES, perm)


CORE = [(0, 1), (0, 0), (0, 3), (0, 2)]
ACROSS = [(0, 2), (0, 3), (0, 0), (0, 1)]


def dot(a, b, ca, cb):
    return lax.dot_general(a, b, (((ca,), (cb,)), ((), ())), preferred_element_type=F32)


def one_hot(index):
    hit = lax.broadcasted_iota(jnp.int32, (TERMS, TERMS), 0) == index
    return jnp.where(hit, 1.0, 0.0).astype(BF16)


def shape(rows, dtype=BF16):
    return jax.ShapeDtypeStruct((rows, TERMS), dtype)


def vmem(rows, dtype=BF16):
    return pltpu.VMEM((rows, TERMS), dtype)


def cost(flops, moved, trans=0):
    return pl.CostEstimate(flops=flops, bytes_accessed=moved, transcendentals=trans)


MATMUL = 2 * WIDE * TERMS * TERMS


def last_rows(emb_ref, tail, rows):
    left = DIM - FULL
    tail[:left] = emb_ref[FULL:DIM].astype(F32)
    for i, row in enumerate(rows):
        tail[left + i : left + i + 1] = row
    return tail[...].astype(BF16)


def order(ref, swap):
    idx = ref[...].reshape(2, TERMS)
    one, two = idx[:1], idx[1:]
    return jnp.where(swap, two, one), jnp.where(swap, one, two)


def pack_kernel(swap_ref, emb_ref, off_ref, idx_ref, out_ref, idx_out, tail):
    idx, idx_2 = order(idx_ref, swap_ref[0] == 1)
    idx_out[...] = idx_2
    zero = jnp.zeros((1, TERMS), F32)
    high = (idx // DIGIT).astype(F32)
    low = (idx % DIGIT).astype(F32)
    off = off_ref[...].astype(F32).reshape(1, TERMS)
    out_ref[:FULL] = emb_ref[:FULL]
    out_ref[FULL:] = last_rows(emb_ref, tail, [off, high, low, zero])


KERNEL_VMEM = 32 * 2**20
VMEM = pl.BlockSpec(memory_space=pltpu.VMEM)
SMEM = pl.BlockSpec(memory_space=pltpu.SMEM)
HBM = pl.BlockSpec(memory_space=pltpu.HBM)


def pack(swap, emb, off, idx):
    return pl.pallas_call(
        pack_kernel,
        out_shape=(shape(WIDE), shape(1, jnp.int32)),
        in_specs=[SMEM] + [VMEM] * 3,
        out_specs=(VMEM,) * 2,
        scratch_shapes=[pltpu.VMEM((16, TERMS), F32)],
        cost_estimate=cost(0, 1300000),
    )(swap, emb, off, idx)


def rows_kernel(swap_ref, emb_ref, off_ref, idx_ref, row_1, row_2, wide, tail):
    zero = jnp.zeros((1, TERMS), F32)
    off = off_ref[...].astype(F32).reshape(1, TERMS)
    wide[:FULL] = emb_ref[:FULL]
    wide[FULL:] = last_rows(emb_ref, tail, [zero + 1.0, off, zero, zero])
    for idx, out in zip(order(idx_ref, swap_ref[0] == 1), (row_1, row_2)):
        out[...] = dot(wide[...], one_hot(idx), 1, 0).astype(BF16)


def pick_rows(swap, emb, off, idx):
    return pl.pallas_call(
        rows_kernel,
        out_shape=(shape(WIDE), shape(WIDE)),
        in_specs=[SMEM] + [VMEM] * 3,
        out_specs=(VMEM,) * 2,
        scratch_shapes=[pltpu.VMEM((WIDE, TERMS), BF16), pltpu.VMEM((16, TERMS), F32)],
        cost_estimate=cost(2 * MATMUL, 2000000),
    )(swap, emb, off, idx)


def cells(score, count):
    scale = 1.0 / TERMS
    count_f = count.astype(F32)
    slope = 0.1 * scale + (0.25 * scale) * (count_f * lax.rsqrt(count_f))
    seen = slope * (score - jnp.log(count_f))
    unseen = 0.5 * scale + (0.5 * scale) * jnp.tanh(0.5 * score)
    return jnp.where(count > 0, seen, unseen).astype(BF16)


def start(src, dst, sem):
    copy = pltpu.make_async_copy(src, dst, sem)
    copy.start()
    return copy


def score(pair, idx, block, counts_ref, row_ref, row_idx, counts, row, cell_buf, sems, then=None):
    get_row = start(row_ref, row, sems.at[0])
    parts = [pl.ds(i * (TERMS // 4), TERMS // 4) for i in range(4)]
    get_counts = [
        start(counts_ref.at[pair, part], counts.at[part], sems.at[4 + i])
        for i, part in enumerate(parts)
    ]
    pick = one_hot(idx)
    col = dot(block, pick, 1, 0)
    at = lax.broadcasted_iota(jnp.int32, (WIDE, TERMS), 0)
    col = jnp.where(at > OFF, jnp.where(at == ONE, 1.0, 0.0), col).astype(BF16)
    get_row.wait()
    est = dot(row[...], col, 0, 0)
    for get in get_counts:
        get.wait()
    if then is not None:
        then()
    cell_buf[...] = cells(est, counts[...])
    grad = dot(row[...], cell_buf[...], 1, 0).astype(BF16)
    grad = dot(grad, pick, 1, 1).astype(BF16)
    row_part = dot(col, cell_buf[...], 1, 1).astype(BF16)
    return grad, dot(row_part, one_hot(row_idx), 1, 1)


SCORE_SCRATCH = [
    pltpu.VMEM((TERMS, TERMS), jnp.int32),
    pltpu.VMEM((WIDE, TERMS), BF16),
    pltpu.VMEM((TERMS, TERMS), BF16),
    pltpu.SemaphoreType.DMA((8,)),
    pltpu.VMEM((WIDE, TERMS), F32),
]


def first_kernel(
    swap_ref, counts_ref, row_ref, row_idx_ref, block_ref, col_out, row_out,
    counts, row, cell_buf, sems, total,
):
    swap = swap_ref[0]
    digits = block_ref[FULL:].astype(F32)
    one = ONE - FULL
    idx = (digits[one : one + 1] * DIGIT + digits[one + 1 : one + 2]).astype(jnp.int32)
    row_idx = order(row_idx_ref, swap == 1)[0]
    grad, total[...] = score(
        swap, idx, block_ref[...], counts_ref, row_ref, row_idx, counts, row, cell_buf, sems
    )
    put = start(total, row_out, sems.at[2])
    col_out[...] = grad
    put.wait()


def first_pair(swap, *args):
    return pl.pallas_call(
        first_kernel,
        out_shape=(vmem(WIDE), pltpu.HBM((WIDE, TERMS), F32)),
        in_specs=[SMEM, HBM, HBM, VMEM, VMEM],
        out_specs=(VMEM, HBM),
        scratch_shapes=SCORE_SCRATCH,
        compiler_params=pltpu.CompilerParams(vmem_limit_bytes=KERNEL_VMEM),
        cost_estimate=cost(6 * MATMUL, 12000000, 3 * TERMS * TERMS),
    )(swap, *args)


def put_halves(value, low_out, high_out):
    low_out[...] = value[:LOW]
    high_out[:HIGH] = value[LOW:]
    high_out[HIGH:] = jnp.zeros((LOW - HIGH, TERMS), BF16)


def second_kernel(
    swap_ref, counts_ref, row_ref, prev_ref, row_idx_ref, idx_ref, block_ref, block_2_ref,
    low_out, high_out, row_low_out, row_high_out, counts, row, cell_buf, sems, prev,
):
    swap = swap_ref[0]
    get_prev = pltpu.make_async_copy(prev_ref, prev, sems.at[2])
    row_idx = order(row_idx_ref, swap == 1)[1]
    block = block_ref[...] + block_2_ref[...]
    grad, total = score(
        1 - swap, idx_ref[...], block, counts_ref, row_ref, row_idx, counts, row, cell_buf, sems,
        get_prev.start,
    )
    low_out[...] = grad[:LOW]
    high_out[...] = grad[LOW:]
    get_prev.wait()
    put_halves((prev[...] + total).astype(BF16), row_low_out, row_high_out)


def second_pair(swap, *args):
    return pl.pallas_call(
        second_kernel,
        out_shape=(vmem(LOW), vmem(HIGH), shape(LOW), shape(LOW)),
        in_specs=[SMEM] + [HBM] * 3 + [VMEM] * 4,
        out_specs=(VMEM,) * 4,
        scratch_shapes=SCORE_SCRATCH,
        compiler_params=pltpu.CompilerParams(vmem_limit_bytes=KERNEL_VMEM),
        cost_estimate=cost(6 * MATMUL, 12000000, 3 * TERMS * TERMS),
    )(swap, *args)


def adagrad(low, high, table, acc):
    total = jnp.concatenate([low, high[: DIM - LOW]]).astype(F32)
    step = LEARN_RATE * total * lax.rsqrt(acc + total * total)
    return (table.astype(F32) - step).astype(BF16)


def in_hbm(array):
    return pltpu.with_memory_space_constraint(array, pltpu.HBM)


def halves(core, low, high):
    return jnp.where(core == 0, low, high), jnp.where(core == 0, high, low)


def add(*parts):
    total = parts[0].astype(F32)
    for part in parts[1:]:
        total = total + part.astype(F32)
    return total.astype(BF16)


def per_device(
    row_emb, col_emb, row_acc, col_acc, row_offset, col_offset, counts, row_index, col_index
):
    replica = lax.axis_index("rep")
    core = replica & 1
    is_0, is_3 = replica == 0, replica == 3
    swap = is_3.astype(jnp.int32).reshape(1)
    counts = in_hbm(counts.reshape(counts.shape[2:]))

    barrier = lax.optimization_barrier
    block, col_idx_2 = pack(swap, col_emb.T, col_offset, col_index)
    got = hop("got", block, [(0, 0), (-1, 1), (-2, 2), (1, 3)])
    far = hop("far", block, [None, (3, 1), None, None])
    idx_2 = hop("idx_2", col_idx_2, [(-4, 0), (3, 1), (2, 2), (-3, 3)])
    row_1, row_2 = pick_rows(swap, row_emb.T, row_offset, row_index)
    got, row_1 = barrier((got, row_1))
    near = hop("near", got, [None, (-3, 0), (-1, 3), (1, 2)])
    grad_1, row_sum = first_pair(swap, counts, in_hbm(row_1), row_index, got)
    near, far, idx_2, grad_1 = barrier((near, far, idx_2, grad_1))
    low, high, row_low, row_high = second_pair(
        swap, counts, in_hbm(row_2), in_hbm(row_sum), row_index, idx_2, far, near
    )

    way = [(3, 1), (-3, 0), (-1, 3), (1, 2)]
    low = hop("low", low, way)
    high = hop("high", high, way)
    row_keep, row_give = halves(core, row_low, row_high)
    row_chip = add(row_keep, hop("row_swap", row_give, CORE))
    row_across = hop("row_across", row_chip, ACROSS)
    high, row_across = barrier((add(grad_1[LOW:], high), row_across))
    low = add(grad_1[:LOW], low)
    low_up = hop("low_up", low, [None, (1, 0), (2, 2), None])
    low_down = hop("low_down", low, [None, None, None, (-1, 2)])
    high_up = hop("high_up", high, [None, (1, 0), (2, 3), None])
    high_down = hop("high_down", high, [None, None, None, (-1, 3)])
    high = add(high_up, high_down, jnp.where(is_0, high, 0))
    high_across = hop("high_across", high, [(0, 3), None, None, (0, 0)])
    high = add(high, high_across)
    high = high + hop("high_other", high, [(0, 1), None, None, (0, 2)])
    low_up, row_across = barrier((low_up, row_across))
    row_mine = add(row_chip, row_across)
    row_other = hop("row_other", row_mine, CORE)
    row_low, row_high = halves(core, row_mine, row_other)
    new_row = adagrad(row_low, row_high, row_emb.T, row_acc.T)

    low = add(low_up, low_down, jnp.where(is_0, low, 0))
    low_across = hop("low_across", low, [(0, 2), None, (0, 0), None])
    low_across, new_row = barrier((low_across, new_row))
    low = add(low, low_across)
    low = low + hop("low_other", low, [(0, 1), None, (0, 3), None])
    new_col = adagrad(low, high, col_emb.T, col_acc.T)
    return (new_row.T, new_col.T)


def solution(mesh):
    in_specs = (
        P("blk", None),
        P("blk", None),
        P("blk", None),
        P("blk", None),
        P("blk"),
        P("blk"),
        P("blk", "rep", None, None, None),
        P("blk", "rep", None, None),
        P("blk", "rep", None, None),
    )
    out_specs = (P("blk", None), P("blk", None))
    return jax.shard_map(
        per_device, mesh=mesh, in_specs=in_specs, out_specs=out_specs, check_vma=False
    )
```
